32 devices in a mesh: front: 4 (over x, core), row: 2 (over y), col: 4 (over z).
Axes of the slice: x: 2, y: 2, z: 4, core: 2. Of those that a mesh axis runs over, the one named last changes fastest.
Arguments:
- parent_entries: float32 [12288, 12288], P('row', ('front', 'col')), as said below
- child_update: float32 [4, 8192, 8192], P('front', 'row', 'col'), as said below
- child_map: int32 [4, 64], replicated, may hold values from 0 to 95, as said below
- child_mask: int32 [4, 64, 64], P('front'), may hold values from 0 to 1, as said below
Outputs:
- schur: float32 [12288, 12288], P('row', ('front', 'col'))
- panel: float32 [12288, 512], P('row')
The draws below stay inside these ranges and needn't reach their ends.
Inputs may be any that keep to these rules, and one draw needn't show every extreme that they name: `child_update`: each child's update matrix is symmetric. `parent_entries`: Symmetric. `child_mask`: symmetric in its last two dimensions, ones on the diagonal. Distinct within each child. With v = j mod (16), e = v mod (8), r = (v mod 16) div (8), k = (v div 16) * 8 + e and g = r * 8 + k div (1), child_map[f, j] div (6) equals g.
All inputs are finite; a program needn't handle non-finite values.
Results may differ from the reference program's by a relative error of at most 0.000071.
Values sent between devices are 32-bit elements; how exact they have to be, the bound alone decides.
A program may use at most 256 MiB of HBM per device.

```python
import math
import jax
import jax.numpy as jnp
from jax import lax

NP = 12288
MC = 8192
W = 512
BLK = 128
GRID_ROWS = 2
GRID_COLS = 4
GROUPS = 16
FRONTS = 4
MB = 64
PB = 96
SPAN = 16


def draw_parent_entries(key, part):
    noise = jax.random.normal(key, (NP, NP), jnp.float32)
    diagonal = jax.random.uniform(jax.random.fold_in(key, 1), (NP,), jnp.float32, 6.0, 9.0)
    mirrored = (noise + noise.T) * 0.70710678
    lines = jnp.arange(NP)
    leading = lines < W
    both_leading = leading[:, None] & leading[None, :]
    one_leading = leading[:, None] != leading[None, :]
    spread = jnp.where(both_leading, 0.8 / math.sqrt(W), jnp.where(one_leading, 2.2 / math.sqrt(NP), 0.5 / math.sqrt(NP)))
    onto = lines[:, None] == lines[None, :]
    return mirrored * spread + jnp.where(onto, diagonal[:, None], 0.0)


def draw_child_update(key, part):
    noise = jax.random.normal(key, (FRONTS, MC, MC), jnp.float32)
    mirrored = (noise + jnp.swapaxes(noise, 1, 2)) * (0.70710678 / math.sqrt(MC))
    return mirrored


def draw_child_mask(key, part):
    values = jax.random.randint(key, (FRONTS, MB, MB), 0, 5)
    keep = jnp.where(values < 3, 1, 0).astype(jnp.int32)
    lines = jnp.arange(MB)
    upper = lines[:, None] <= lines[None, :]
    mirrored = jnp.where(upper[None], keep, jnp.swapaxes(keep, 1, 2))
    onto = lines[:, None] == lines[None, :]
    return jnp.where(onto[None], 1, mirrored).astype(jnp.int32)


def draw_child_map(key, part):
    blocks = jnp.arange(MB, dtype=jnp.int32)
    column_blocks = MB // GRID_COLS
    share = SPAN // GRID_ROWS
    within = blocks % column_blocks
    row_part = within % SPAN // share
    rank_part = within // SPAN * share + within % SPAN % share
    target = row_part * (GROUPS // GRID_ROWS) + rank_part // (column_blocks // GROUPS)
    earlier = (target[:, None] == target[None, :]) & (blocks[None, :] < blocks[:, None])
    order = jnp.sum(earlier.astype(jnp.int32), axis=1)
    slots = PB // GROUPS
    scores = jax.random.randint(key, (FRONTS, GROUPS, slots), 0, 1 << 20) * slots + jnp.arange(slots, dtype=jnp.int32)
    shuffled = jnp.argsort(scores, axis=-1).astype(jnp.int32)
    chosen = shuffled[:, target, order]
    return (target[None, :] * slots + chosen).astype(jnp.int32)


def setup_inputs(seed: int = 0) -> dict:
    streams_of = jax.random.split(jax.random.key(seed), 5)
    parent_entries = draw_parent_entries(jax.random.fold_in(streams_of[4], 71), 0)
    child_update = draw_child_update(jax.random.fold_in(streams_of[4], 71), 0)
    child_map = draw_child_map(jax.random.fold_in(streams_of[4], 71), 0)
    child_mask = draw_child_mask(jax.random.fold_in(streams_of[4], 71), 0)
    return dict(parent_entries=parent_entries, child_update=child_update, child_map=child_map, child_mask=child_mask)


def reference(parent_entries, child_update, child_map, child_mask):
    front = parent_entries
    offsets = jnp.arange(BLK, dtype=jnp.int32)
    for child in range(FRONTS):
        spread = jnp.repeat(jnp.repeat(child_mask[child], BLK, axis=0), BLK, axis=1)
        masked = child_update[child] * spread.astype(child_update.dtype)
        places = (child_map[child][:, None] * BLK + offsets[None, :]).reshape(-1).astype(jnp.int32)
        front = front.at[places[:, None], places[None, :]].add(masked)
    factor = jnp.linalg.cholesky(front[:W, :W])
    panel = jax.scipy.linalg.solve_triangular(factor, front[:, :W].T, lower=True).T
    schur = front - jnp.dot(panel, panel.T, precision=lax.Precision.HIGHEST)
    lines = jnp.arange(NP)
    keep = (lines[:, None] >= W) & (lines[None, :] >= W)
    schur = jnp.where(keep, schur, jnp.zeros_like(schur))
    return (schur, panel)
```

```python
import functools

import jax
import jax.numpy as jnp
from jax import lax
from jax.experimental import pallas as pl
from jax.experimental.pallas import tpu as pltpu
from jax.sharding import PartitionSpec as P

W = 512
BLK = 128
MESH = pl.DeviceIdType.MESH
HIGHEST = lax.Precision.HIGHEST


class Sizes:
    def __init__(self, mesh, child_rows, child_cols):
        self.fronts = mesh.shape["front"]
        self.rows = mesh.shape["row"]
        self.cols = mesh.shape["col"]
        self.groups = self.fronts * self.cols
        self.row_blocks = child_rows // BLK
        self.period = child_cols // BLK
        self.span = min(self.row_blocks, self.period)
        self.share = self.span // self.rows
        self.ratio = self.groups // self.rows
        self.parts = self.period // self.span
        self.units = self.row_blocks // self.span
        self.holds = max(1, self.row_blocks // self.period)


def rank(place, target, cols):
    away = jnp.abs(place - target)
    low = jnp.where(place > target, 1, 0)
    high = jnp.where(place < target, 1, 0)
    return 2 * away + jnp.where(target * 2 < cols, low, high)


def exchange_kernel(s, lead, child_ref, mask_ref, direct_ref, turned_ref, *rest):
    if lead:
        masks_ref, send_sem, recv_sem, mask_sem = rest
    else:
        send_sem, recv_sem = rest
    f = lax.axis_index("front")
    r = lax.axis_index("row")
    z = lax.axis_index("col")
    devices = s.groups * s.rows
    me = (f * s.rows + r) * s.cols + z
    targets = s.groups if lead else devices
    height = BLK if lead else s.share * BLK
    parts = 1 if lead else s.parts

    def place(step):
        other = lax.rem(me + step, devices)
        return other // (s.rows * s.cols), other // s.cols % s.rows, other % s.cols

    barrier = pltpu.get_barrier_semaphore()

    @pl.loop(1, devices)
    def greet(step):
        tf, tr, tz = place(step)
        pl.semaphore_signal(barrier, inc=1, device_id=(tf, tr, tz), device_id_type=MESH)

    pl.semaphore_wait(barrier, devices - 1)

    def lead_place(step):
        spot = f * s.cols + z
        other = lax.rem(spot + step, s.groups)
        return other // s.cols, 0, other % s.cols

    def visit(step, act):
        tf, tr, tz = lead_place(step) if lead else place(step)
        group = tf * s.cols + tz
        k = group % s.ratio
        v = k // s.share * s.span + group // s.ratio * s.share + k % s.share
        own = (tf == f) & (tr == r) & (tz == z)
        near = rank(z, tz, s.cols)
        for t in range(s.units):
            u = r * s.units + t
            a, h = u // s.parts, u % s.parts
            chosen = near <= rank(a, tz, s.cols)
            if lead:
                chosen = chosen & (h == 0)
            source = child_ref.at[
                pl.ds(pl.multiple_of((t * s.span + tr * s.share) * BLK, BLK), height),
                pl.ds(pl.multiple_of(v * BLK, BLK), BLK),
            ]
            target = direct_ref.at[f, z, a, h]
            act(chosen, own, source, target, (tf, tr, tz), step, t, (z, a, h))
        for t in range(s.holds):
            c = r * s.row_blocks // s.period + t
            line = s.period * c + v - r * s.row_blocks
            held = (line >= 0) & (line < s.row_blocks)
            chosen = held & (near < rank(c, tz, s.cols))
            line = jnp.clip(line, 0, s.row_blocks - 1)
            for h in range(parts):
                source = child_ref.at[
                    pl.ds(pl.multiple_of(line * BLK, BLK), BLK),
                    pl.ds(pl.multiple_of((h * s.span + tr * s.share) * BLK, BLK), height),
                ]
                target = turned_ref.at[f, c, z, h]
                number = s.units + t * parts + h
                act(chosen, own, source, target, (tf, tr, tz), step, number, (c, z, h))

    def slot_of(c, a, h):
        return ((f * s.cols + c) * s.cols + a) * parts + h

    def start(chosen, own, source, target, where, step, number, unit):
        recv = recv_sem.at[slot_of(*unit)]

        @pl.when(chosen & own)
        def _():
            pltpu.make_async_copy(source, target, recv).start()

        @pl.when(chosen & jnp.logical_not(own))
        def _():
            pltpu.make_async_remote_copy(
                src_ref=source,
                dst_ref=target,
                send_sem=send_sem.at[step, number],
                recv_sem=recv,
                device_id=where,
                device_id_type=MESH,
            ).start()

    def finish(chosen, own, source, target, where, step, number, unit):
        @pl.when(chosen & jnp.logical_not(own))
        def _():
            pltpu.make_async_copy(source, target, send_sem.at[step, number]).wait()

    @pl.loop(0, targets)
    def send(step):
        visit(step, start)

    if lead:
        def mask_copy(hop):
            return pltpu.make_async_remote_copy(
                src_ref=mask_ref.at[0],
                dst_ref=masks_ref.at[f],
                send_sem=mask_sem.at[0, hop],
                recv_sem=mask_sem.at[1, hop],
                device_id=(lax.rem(f + hop, s.fronts), r, z),
                device_id_type=MESH,
            )

        for hop in range(1, s.fronts):
            mask_copy(hop).start()
        own_mask = pltpu.make_async_copy(mask_ref.at[0], masks_ref.at[f], mask_sem.at[0, 0])
        own_mask.start()
        own_mask.wait()
        for hop in range(1, s.fronts):
            mask_copy(hop).wait()

    def arrive():
        @pl.loop(0, s.fronts * s.cols * s.cols * parts)
        def wait(slot):
            first = direct_ref.at[0, 0, 0, 0]
            pltpu.make_async_copy(first, first, recv_sem.at[slot]).wait()

    if lead:
        pl.when(r == 0)(arrive)
    else:
        arrive()

    @pl.loop(0, targets)
    def drain(step):
        visit(step, finish)


def exchange(s, lead, child, mask):
    parts = 1 if lead else s.parts
    height = BLK if lead else s.share * BLK
    targets = s.groups if lead else s.groups * s.rows
    shapes = [
        jax.ShapeDtypeStruct((s.fronts, s.cols, s.cols, parts, height, BLK), jnp.float32),
        jax.ShapeDtypeStruct((s.fronts, s.cols, s.cols, parts, BLK, height), jnp.float32),
    ]
    scratch = [
        pltpu.SemaphoreType.DMA((targets, s.units + s.holds * parts)),
        pltpu.SemaphoreType.DMA((s.fronts * s.cols * s.cols * parts,)),
    ]
    if lead:
        shapes.append(jax.ShapeDtypeStruct((s.fronts,) + mask.shape[1:], jnp.int32))
        scratch.append(pltpu.SemaphoreType.DMA((2, s.fronts)))
    return pl.pallas_call(
        functools.partial(exchange_kernel, s, lead),
        out_shape=shapes,
        in_specs=[pl.BlockSpec(memory_space=pl.ANY)] * 2,
        out_specs=[pl.BlockSpec(memory_space=pl.ANY)] * len(shapes),
        scratch_shapes=scratch,
        compiler_params=pltpu.CompilerParams(
            collective_id=0 if lead else 1, has_side_effects=True
        ),
        name="lead_exchange" if lead else "exchange",
    )(child, mask)


def assemble(s, table_ref, chunk, parent_ref, direct_ref, turned_ref, front_ref, slots):
    @pl.loop(0, slots * slots)
    def block(spot):
        i, j = spot // slots, spot % slots
        rows = pl.ds(pl.multiple_of(i * BLK, BLK), BLK)
        cols = pl.ds(pl.multiple_of(j * BLK, BLK), BLK)
        front_ref[rows, cols] = parent_ref[rows, cols]
        for f in range(s.fronts):
            code = table_ref[((chunk * slots + i) * slots + j) * s.fronts + f]
            unit = jnp.maximum(code - 1, 0) // 2
            c, a = unit // s.cols, unit % s.cols

            @pl.when((code > 0) & (code % 2 == 1))
            def _():
                front_ref[rows, cols] += direct_ref[f, c, a, 0]

            @pl.when((code > 0) & (code % 2 == 0))
            def _():
                front_ref[rows, cols] += turned_ref[f, c, a, 0].T


def lead_kernel(s, slots, table_ref, parent_ref, direct_ref, turned_ref, front_ref):
    assemble(s, table_ref, 0, parent_ref, direct_ref, turned_ref, front_ref, slots)


def assemble_lead(s, slots, table, parent, direct, turned):
    side = slots * BLK
    blocks = (s.fronts, s.cols, s.cols, 1, BLK, BLK)
    return pl.pallas_call(
        functools.partial(lead_kernel, s, slots),
        grid_spec=pltpu.PrefetchScalarGridSpec(
            num_scalar_prefetch=1,
            grid=(1,),
            in_specs=[
                pl.BlockSpec((side, side), lambda k, t: (0, 0)),
                pl.BlockSpec(blocks, lambda k, t: (0,) * 6),
                pl.BlockSpec(blocks, lambda k, t: (0,) * 6),
            ],
            out_specs=pl.BlockSpec((side, side), lambda k, t: (0, 0)),
        ),
        out_shape=jax.ShapeDtypeStruct((side, side), jnp.float32),
        compiler_params=pltpu.CompilerParams(vmem_limit_bytes=48 << 20),
        name="assemble_lead",
    )(table, parent, direct, turned)


def dot(x, y):
    return lax.dot_general(
        x, y, (((1,), (0,)), ((), ())), precision=HIGHEST, preferred_element_type=jnp.float32
    )


def dot_turned(x, y):
    return lax.dot_general(
        x, y, (((1,), (1,)), ((), ())), precision=HIGHEST, preferred_element_type=jnp.float32
    )


def invert_kernel(corner_ref, right_ref, out_ref, work, lower, eliminate, gather):
    count = W // BLK
    work[...] = corner_ref[...]
    line = lax.broadcasted_iota(jnp.int32, (BLK, 1), 0)
    lane = lax.broadcasted_iota(jnp.int32, (BLK, BLK), 1)
    for b in range(count):
        here = slice(b * BLK, (b + 1) * BLK)
        eliminate[...] = work[here, here]
        gather[...] = jnp.where(line == lane, 1.0, 0.0)

        @pl.loop(0, BLK)
        def step(j):
            block = eliminate[...]
            pivot_row = eliminate[pl.ds(j, 1), :]
            identity_row = gather[pl.ds(j, 1), :]
            column = jnp.sum(jnp.where(lane == j, block, 0.0), axis=1, keepdims=True)
            pivot = jnp.sum(jnp.where(line == j, column, 0.0), axis=0, keepdims=True)
            root = lax.rsqrt(pivot)
            root = root * (1.5 - 0.5 * pivot * root * root)
            scale = jnp.where(line > j, column / pivot, 0.0)
            keep = jnp.where(line == j, root, 1.0)
            eliminate[...] = block - scale * pivot_row
            gather[...] = (gather[...] - scale * identity_row) * keep

        inverse = gather[...]
        if b + 1 < count:
            below = slice((b + 1) * BLK, W)
            panel = dot_turned(work[below, here], inverse)
            lower[below, here] = panel
            work[below, below] = work[below, below] - dot_turned(panel, panel)
        total = right_ref[here, :]
        if b:
            total = total - dot(lower[here, 0 : b * BLK], out_ref[0 : b * BLK, :])
        out_ref[here, :] = dot(inverse, total)


def solve(corner, right):
    return pl.pallas_call(
        invert_kernel,
        out_shape=jax.ShapeDtypeStruct(right.shape, jnp.float32),
        scratch_shapes=[
            pltpu.VMEM((W, W), jnp.float32),
            pltpu.VMEM((W, W), jnp.float32),
            pltpu.VMEM((BLK, BLK), jnp.float32),
            pltpu.VMEM((BLK, BLK), jnp.float32),
        ],
        compiler_params=pltpu.CompilerParams(vmem_limit_bytes=48 << 20),
        name="factor_and_solve",
    )(corner, right)


def schur_kernel(s, slots, table_ref, place_ref, parent_ref, direct_ref, turned_ref, across_ref, *rest):
    pieces = rest[: s.rows]
    schur_ref, panel_ref, front = rest[s.rows :]
    k = pl.program_id(0)
    assemble(s, table_ref, k, parent_ref, direct_ref, turned_ref, front, slots)
    part = slots * BLK // s.rows
    for n in range(s.rows):
        panel_ref[n * part : (n + 1) * part, :] = pieces[n][0]
    side = slots * BLK
    product = dot_turned(panel_ref[...], across_ref[...])
    rows = place_ref[0] + k * side + lax.broadcasted_iota(jnp.int32, (side, 1), 0)
    cols = place_ref[1] + lax.broadcasted_iota(jnp.int32, (1, side), 1)
    schur_ref[...] = jnp.where((rows >= W) & (cols >= W), front[...] - product, 0.0)


def assemble_schur(s, slots, table, place, parent, direct, turned, across, gathered):
    side = slots * BLK
    steps = parent.shape[0] // side
    part = side // s.rows
    blocks = (s.fronts, s.cols, s.cols, 1, BLK, BLK)
    return pl.pallas_call(
        functools.partial(schur_kernel, s, slots),
        grid_spec=pltpu.PrefetchScalarGridSpec(
            num_scalar_prefetch=2,
            grid=(steps,),
            in_specs=[
                pl.BlockSpec((side, side), lambda k, t, p: (k, 0)),
                pl.BlockSpec(blocks, lambda k, t, p: (0, 0, 0, k // s.share, k % s.share, 0)),
                pl.BlockSpec(blocks, lambda k, t, p: (0, 0, 0, k // s.share, 0, k % s.share)),
                pl.BlockSpec((side, W), lambda k, t, p: (0, 0)),
            ]
            + [
                pl.BlockSpec((1, part, W), functools.partial(lambda n, k, t, p: (n * s.ratio + k, 0, 0), n))
                for n in range(s.rows)
            ],
            out_specs=[
                pl.BlockSpec((side, side), lambda k, t, p: (k, 0)),
                pl.BlockSpec((side, W), lambda k, t, p: (k, 0)),
            ],
            scratch_shapes=[pltpu.VMEM((side, side), jnp.float32)],
        ),
        out_shape=[
            jax.ShapeDtypeStruct(parent.shape, jnp.float32),
            jax.ShapeDtypeStruct((parent.shape[0], W), jnp.float32),
        ],
        compiler_params=pltpu.CompilerParams(vmem_limit_bytes=56 << 20),
        name="assemble_schur",
    )(table, place, parent, direct, turned, across, *([gathered] * s.rows))


def body(mesh, parent_entries, child_update, child_map, child_mask):
    child = child_update[0]
    s = Sizes(mesh, *child.shape)
    row_index = lax.axis_index("row")
    column_index = lax.axis_index("col")
    group_index = lax.axis_index(("front", "col"))
    front_rows, front_cols = parent_entries.shape
    slots = front_cols // BLK

    lead_direct, lead_turned, masks = exchange(s, True, child, child_mask)

    def sources(first, count):
        places = first + jnp.arange(count, dtype=jnp.int32)
        return child_map[:, None, :] == places[None, :, None]

    on_rows = sources(row_index * (front_rows // BLK), front_rows // BLK)
    on_cols = sources(group_index * slots, slots)
    kept = jnp.einsum(
        "fap,fpq,fbq->abf",
        on_rows.astype(jnp.float32),
        masks.astype(jnp.float32),
        on_cols.astype(jnp.float32),
    )
    numbers = jnp.arange(child_map.shape[1], dtype=jnp.int32) // s.period
    row_unit = jnp.sum(jnp.where(on_rows, numbers, 0), axis=-1).T[:, None, :]
    col_unit = jnp.sum(jnp.where(on_cols, numbers, 0), axis=-1).T[None, :, :]
    straight = rank(col_unit, column_index, s.cols) <= rank(row_unit, column_index, s.cols)
    code = 1 + 2 * (col_unit * s.cols + row_unit) + jnp.where(straight, 0, 1)
    table = jnp.where(kept > 0.5, code, 0).astype(jnp.int32).reshape(-1)

    lead = assemble_lead(s, slots, table, parent_entries, lead_direct, lead_turned)[:W]
    corner = lax.psum(jnp.where(group_index == 0, lead[:, :W], 0.0), ("front", "col"))
    solved = solve(corner, lead)
    piece = solved.T
    across = piece
    for r in range(1, s.rows):
        moved = lax.ppermute(piece, "row", [(0, r)])
        across = jnp.where(row_index == r, moved, across)

    part = front_cols // s.rows
    mine = lax.dynamic_slice_in_dim(across, row_index * part, part, 0)
    slot = mine
    owner = group_index // s.ratio
    for shift in range(1, s.rows):
        wanted = lax.rem(row_index + shift, s.rows)
        pairs = []
        for r in range(s.rows):
            for k in range(s.ratio):
                a, b = s.ratio * r + k, s.ratio * ((r + shift) % s.rows) + k
                index = [(g // s.cols * s.rows + r) * s.cols + g % s.cols for g in (a, b)]
                pairs.append(tuple(index))
        sent = lax.dynamic_slice_in_dim(across, wanted * part, part, 0)
        got = lax.ppermute(sent, ("front", "row", "col"), pairs)
        slot = jnp.where(owner == wanted, got, slot)
    gathered = lax.all_gather(slot, ("front", "col"))

    direct, turned = exchange(s, False, child, child_mask)
    place = jnp.stack([row_index * front_rows, group_index * front_cols]).astype(jnp.int32)
    return tuple(
        assemble_schur(
            s, slots, table, place, parent_entries, direct, turned, across, gathered
        )
    )


def solution(mesh):
    placed = (P("row", ("front", "col")), P("front", "row", "col"), P(), P("front", None, None))
    return jax.shard_map(
        functools.partial(body, mesh),
        mesh=mesh,
        in_specs=placed,
        out_specs=(P("row", ("front", "col")), P("row", None)),
        check_vma=False,
    )
```

```python
import functools

import jax
import jax.numpy as jnp
from jax import lax
from jax.experimental import pallas as pl
from jax.experimental.pallas import tpu as pltpu
from jax.sharding import PartitionSpec as P

W = 512
BLK = 128
MESH = pl.DeviceIdType.MESH
HIGHEST = lax.Precision.HIGHEST


class Sizes:
    def __init__(self, mesh, child_rows, child_cols):
        self.fronts = mesh.shape["front"]
        self.rows = mesh.shape["row"]
        self.cols = mesh.shape["col"]
        self.groups = self.fronts * self.cols
        self.row_blocks = child_rows // BLK
        self.period = child_cols // BLK
        self.span = min(self.row_blocks, self.period)
        self.share = self.span // self.rows
        self.ratio = self.groups // self.rows
        self.parts = self.period // self.span
        self.units = self.row_blocks // self.span
        self.holds = max(1, self.row_blocks // self.period)


def rank(place, target, cols):
    away = jnp.abs(place - target)
    low = jnp.where(place > target, 1, 0)
    high = jnp.where(place < target, 1, 0)
    return 2 * away + jnp.where(target * 2 < cols, low, high)


def exchange_kernel(s, lead, child_ref, mask_ref, direct_ref, turned_ref, *rest):
    if lead:
        masks_ref, send_sem, recv_sem, mask_sem = rest
    else:
        send_sem, recv_sem = rest
    f = lax.axis_index("front")
    r = lax.axis_index("row")
    z = lax.axis_index("col")
    devices = s.groups * s.rows
    targets = s.groups if lead else devices
    height = BLK if lead else s.share * BLK
    parts = 1 if lead else s.parts

    def place(step):
        dz, turn = step % s.cols, step // s.cols
        df, dr = (turn + dz) % s.fronts, (turn // s.fronts + dz) % s.rows
        return lax.rem(f + df, s.fronts), lax.rem(r + dr, s.rows), lax.rem(z + dz, s.cols)

    barrier = pltpu.get_barrier_semaphore()

    @pl.loop(1, devices)
    def greet(step):
        tf, tr, tz = place(step)
        pl.semaphore_signal(barrier, inc=1, device_id=(tf, tr, tz), device_id_type=MESH)

    pl.semaphore_wait(barrier, devices - 1)

    def lead_place(step):
        dz = step % s.cols
        df = (step // s.cols + dz) % s.fronts
        return lax.rem(f + df, s.fronts), 0, lax.rem(z + dz, s.cols)

    def visit(step, act):
        tf, tr, tz = lead_place(step) if lead else place(step)
        group = tf * s.cols + tz
        k = group % s.ratio
        v = k // s.share * s.span + group // s.ratio * s.share + k % s.share
        own = (tf == f) & (tr == r) & (tz == z)
        near = rank(z, tz, s.cols)
        for t in range(s.units):
            u = r * s.units + t
            a, h = u // s.parts, u % s.parts
            chosen = near <= rank(a, tz, s.cols)
            if lead:
                chosen = chosen & (h == 0)
            source = child_ref.at[
                pl.ds(pl.multiple_of((t * s.span + tr * s.share) * BLK, BLK), height),
                pl.ds(pl.multiple_of(v * BLK, BLK), BLK),
            ]
            target = direct_ref.at[f, z, a, h]
            act(chosen, own, source, target, (tf, tr, tz), step, t, (z, a, h))
        for t in range(s.holds):
            c = r * s.row_blocks // s.period + t
            line = s.period * c + v - r * s.row_blocks
            held = (line >= 0) & (line < s.row_blocks)
            chosen = held & (near < rank(c, tz, s.cols))
            line = jnp.clip(line, 0, s.row_blocks - 1)
            for h in range(parts):
                source = child_ref.at[
                    pl.ds(pl.multiple_of(line * BLK, BLK), BLK),
                    pl.ds(pl.multiple_of((h * s.span + tr * s.share) * BLK, BLK), height),
                ]
                target = turned_ref.at[f, c, z, h]
                number = s.units + t * parts + h
                act(chosen, own, source, target, (tf, tr, tz), step, number, (c, z, h))

    def slot_of(c, a, h):
        return ((f * s.cols + c) * s.cols + a) * parts + h

    def start(chosen, own, source, target, where, step, number, unit):
        recv = recv_sem.at[slot_of(*unit)]

        @pl.when(chosen & own)
        def _():
            pltpu.make_async_copy(source, target, recv).start()

        @pl.when(chosen & jnp.logical_not(own))
        def _():
            pltpu.make_async_remote_copy(
                src_ref=source,
                dst_ref=target,
                send_sem=send_sem.at[step, number],
                recv_sem=recv,
                device_id=where,
                device_id_type=MESH,
            ).start()

    def finish(chosen, own, source, target, where, step, number, unit):
        @pl.when(chosen & jnp.logical_not(own))
        def _():
            pltpu.make_async_copy(source, target, send_sem.at[step, number]).wait()

    @pl.loop(0, targets)
    def send(step):
        visit(step, start)

    if lead:
        def mask_copy(hop):
            return pltpu.make_async_remote_copy(
                src_ref=mask_ref.at[0],
                dst_ref=masks_ref.at[f],
                send_sem=mask_sem.at[0, hop],
                recv_sem=mask_sem.at[1, hop],
                device_id=(lax.rem(f + hop, s.fronts), r, z),
                device_id_type=MESH,
            )

        for hop in range(1, s.fronts):
            mask_copy(hop).start()
        own_mask = pltpu.make_async_copy(mask_ref.at[0], masks_ref.at[f], mask_sem.at[0, 0])
        own_mask.start()
        own_mask.wait()
        for hop in range(1, s.fronts):
            mask_copy(hop).wait()

    def arrive():
        @pl.loop(0, s.fronts * s.cols * s.cols * parts)
        def wait(slot):
            first = direct_ref.at[0, 0, 0, 0]
            pltpu.make_async_copy(first, first, recv_sem.at[slot]).wait()

    if lead:
        pl.when(r == 0)(arrive)
    else:
        arrive()

    @pl.loop(0, targets)
    def drain(step):
        visit(step, finish)


def exchange(s, lead, child, mask):
    parts = 1 if lead else s.parts
    height = BLK if lead else s.share * BLK
    targets = s.groups if lead else s.groups * s.rows
    shapes = [
        jax.ShapeDtypeStruct((s.fronts, s.cols, s.cols, parts, height, BLK), jnp.float32),
        jax.ShapeDtypeStruct((s.fronts, s.cols, s.cols, parts, BLK, height), jnp.float32),
    ]
    scratch = [
        pltpu.SemaphoreType.DMA((targets, s.units + s.holds * parts)),
        pltpu.SemaphoreType.DMA((s.fronts * s.cols * s.cols * parts,)),
    ]
    if lead:
        shapes.append(jax.ShapeDtypeStruct((s.fronts,) + mask.shape[1:], jnp.int32))
        scratch.append(pltpu.SemaphoreType.DMA((2, s.fronts)))
    return pl.pallas_call(
        functools.partial(exchange_kernel, s, lead),
        out_shape=shapes,
        in_specs=[pl.BlockSpec(memory_space=pl.ANY)] * 2,
        out_specs=[pl.BlockSpec(memory_space=pl.ANY)] * len(shapes),
        scratch_shapes=scratch,
        compiler_params=pltpu.CompilerParams(
            collective_id=0 if lead else 1, has_side_effects=True
        ),
        name="lead_exchange" if lead else "exchange",
    )(child, mask)


def assemble(s, table_ref, chunk, parent_ref, direct_ref, turned_ref, front_ref, slots):
    @pl.loop(0, slots * slots)
    def block(spot):
        i, j = spot // slots, spot % slots
        rows = pl.ds(pl.multiple_of(i * BLK, BLK), BLK)
        cols = pl.ds(pl.multiple_of(j * BLK, BLK), BLK)
        front_ref[rows, cols] = parent_ref[rows, cols]
        for f in range(s.fronts):
            code = table_ref[((chunk * slots + i) * slots + j) * s.fronts + f]
            unit = jnp.maximum(code - 1, 0) // 2
            c, a = unit // s.cols, unit % s.cols

            @pl.when((code > 0) & (code % 2 == 1))
            def _():
                front_ref[rows, cols] += direct_ref[f, c, a, 0]

            @pl.when((code > 0) & (code % 2 == 0))
            def _():
                front_ref[rows, cols] += turned_ref[f, c, a, 0].T


def lead_kernel(s, slots, table_ref, parent_ref, direct_ref, turned_ref, front_ref):
    assemble(s, table_ref, 0, parent_ref, direct_ref, turned_ref, front_ref, slots)


def assemble_lead(s, slots, table, parent, direct, turned):
    side = slots * BLK
    blocks = (s.fronts, s.cols, s.cols, 1, BLK, BLK)
    return pl.pallas_call(
        functools.partial(lead_kernel, s, slots),
        grid_spec=pltpu.PrefetchScalarGridSpec(
            num_scalar_prefetch=1,
            grid=(1,),
            in_specs=[
                pl.BlockSpec((side, side), lambda k, t: (0, 0)),
                pl.BlockSpec(blocks, lambda k, t: (0,) * 6),
                pl.BlockSpec(blocks, lambda k, t: (0,) * 6),
            ],
            out_specs=pl.BlockSpec((side, side), lambda k, t: (0, 0)),
        ),
        out_shape=jax.ShapeDtypeStruct((side, side), jnp.float32),
        compiler_params=pltpu.CompilerParams(vmem_limit_bytes=48 << 20),
        name="assemble_lead",
    )(table, parent, direct, turned)


def dot(x, y):
    return lax.dot_general(
        x, y, (((1,), (0,)), ((), ())), precision=HIGHEST, preferred_element_type=jnp.float32
    )


def dot_turned(x, y):
    return lax.dot_general(
        x, y, (((1,), (1,)), ((), ())), precision=HIGHEST, preferred_element_type=jnp.float32
    )


def invert_kernel(corner_ref, right_ref, out_ref, work, lower, eliminate, gather):
    count = W // BLK
    work[...] = corner_ref[...]
    line = lax.broadcasted_iota(jnp.int32, (BLK, 1), 0)
    lane = lax.broadcasted_iota(jnp.int32, (BLK, BLK), 1)
    for b in range(count):
        here = slice(b * BLK, (b + 1) * BLK)
        eliminate[...] = work[here, here]
        gather[...] = jnp.where(line == lane, 1.0, 0.0)

        @pl.loop(0, BLK)
        def step(j):
            block = eliminate[...]
            pivot_row = eliminate[pl.ds(j, 1), :]
            identity_row = gather[pl.ds(j, 1), :]
            column = jnp.sum(jnp.where(lane == j, block, 0.0), axis=1, keepdims=True)
            pivot = jnp.sum(jnp.where(line == j, column, 0.0), axis=0, keepdims=True)
            root = lax.rsqrt(pivot)
            root = root * (1.5 - 0.5 * pivot * root * root)
            scale = jnp.where(line > j, column / pivot, 0.0)
            keep = jnp.where(line == j, root, 1.0)
            eliminate[...] = block - scale * pivot_row
            gather[...] = (gather[...] - scale * identity_row) * keep

        inverse = gather[...]
        if b + 1 < count:
            below = slice((b + 1) * BLK, W)
            panel = dot_turned(work[below, here], inverse)
            lower[below, here] = panel
            work[below, below] = work[below, below] - dot_turned(panel, panel)
        total = right_ref[here, :]
        if b:
            total = total - dot(lower[here, 0 : b * BLK], out_ref[0 : b * BLK, :])
        out_ref[here, :] = dot(inverse, total)


def solve(corner, right):
    return pl.pallas_call(
        invert_kernel,
        out_shape=jax.ShapeDtypeStruct(right.shape, jnp.float32),
        scratch_shapes=[
            pltpu.VMEM((W, W), jnp.float32),
            pltpu.VMEM((W, W), jnp.float32),
            pltpu.VMEM((BLK, BLK), jnp.float32),
            pltpu.VMEM((BLK, BLK), jnp.float32),
        ],
        compiler_params=pltpu.CompilerParams(vmem_limit_bytes=48 << 20),
        name="factor_and_solve",
    )(corner, right)


def schur_kernel(s, slots, table_ref, place_ref, parent_ref, direct_ref, turned_ref, across_ref, *rest):
    pieces = rest[: s.rows]
    schur_ref, panel_ref, front = rest[s.rows :]
    k = pl.program_id(0)
    assemble(s, table_ref, k, parent_ref, direct_ref, turned_ref, front, slots)
    part = slots * BLK // s.rows
    for n in range(s.rows):
        panel_ref[n * part : (n + 1) * part, :] = pieces[n][0]
    side = slots * BLK
    product = dot_turned(panel_ref[...], across_ref[...])
    rows = place_ref[0] + k * side + lax.broadcasted_iota(jnp.int32, (side, 1), 0)
    cols = place_ref[1] + lax.broadcasted_iota(jnp.int32, (1, side), 1)
    schur_ref[...] = jnp.where((rows >= W) & (cols >= W), front[...] - product, 0.0)


def assemble_schur(s, slots, table, place, parent, direct, turned, across, gathered):
    side = slots * BLK
    steps = parent.shape[0] // side
    part = side // s.rows
    blocks = (s.fronts, s.cols, s.cols, 1, BLK, BLK)
    return pl.pallas_call(
        functools.partial(schur_kernel, s, slots),
        grid_spec=pltpu.PrefetchScalarGridSpec(
            num_scalar_prefetch=2,
            grid=(steps,),
            in_specs=[
                pl.BlockSpec((side, side), lambda k, t, p: (k, 0)),
                pl.BlockSpec(blocks, lambda k, t, p: (0, 0, 0, k // s.share, k % s.share, 0)),
                pl.BlockSpec(blocks, lambda k, t, p: (0, 0, 0, k // s.share, 0, k % s.share)),
                pl.BlockSpec((side, W), lambda k, t, p: (0, 0)),
            ]
            + [
                pl.BlockSpec((1, part, W), functools.partial(lambda n, k, t, p: (n * s.ratio + k, 0, 0), n))
                for n in range(s.rows)
            ],
            out_specs=[
                pl.BlockSpec((side, side), lambda k, t, p: (k, 0)),
                pl.BlockSpec((side, W), lambda k, t, p: (k, 0)),
            ],
            scratch_shapes=[pltpu.VMEM((side, side), jnp.float32)],
        ),
        out_shape=[
            jax.ShapeDtypeStruct(parent.shape, jnp.float32),
            jax.ShapeDtypeStruct((parent.shape[0], W), jnp.float32),
        ],
        compiler_params=pltpu.CompilerParams(vmem_limit_bytes=56 << 20),
        name="assemble_schur",
    )(table, place, parent, direct, turned, across, *([gathered] * s.rows))


def body(mesh, parent_entries, child_update, child_map, child_mask):
    child = child_update[0]
    s = Sizes(mesh, *child.shape)
    row_index = lax.axis_index("row")
    column_index = lax.axis_index("col")
    group_index = lax.axis_index(("front", "col"))
    front_rows, front_cols = parent_entries.shape
    slots = front_cols // BLK

    lead_direct, lead_turned, masks = exchange(s, True, child, child_mask)

    def sources(first, count):
        places = first + jnp.arange(count, dtype=jnp.int32)
        return child_map[:, None, :] == places[None, :, None]

    on_rows = sources(row_index * (front_rows // BLK), front_rows // BLK)
    on_cols = sources(group_index * slots, slots)
    kept = jnp.einsum(
        "fap,fpq,fbq->abf",
        on_rows.astype(jnp.float32),
        masks.astype(jnp.float32),
        on_cols.astype(jnp.float32),
    )
    numbers = jnp.arange(child_map.shape[1], dtype=jnp.int32) // s.period
    row_unit = jnp.sum(jnp.where(on_rows, numbers, 0), axis=-1).T[:, None, :]
    col_unit = jnp.sum(jnp.where(on_cols, numbers, 0), axis=-1).T[None, :, :]
    straight = rank(col_unit, column_index, s.cols) <= rank(row_unit, column_index, s.cols)
    code = 1 + 2 * (col_unit * s.cols + row_unit) + jnp.where(straight, 0, 1)
    table = jnp.where(kept > 0.5, code, 0).astype(jnp.int32).reshape(-1)

    lead = assemble_lead(s, slots, table, parent_entries, lead_direct, lead_turned)[:W]
    corner = lax.psum(jnp.where(group_index == 0, lead[:, :W], 0.0), ("front", "col"))
    solved = solve(corner, lead)
    piece = solved.T
    across = piece
    for r in range(1, s.rows):
        moved = lax.ppermute(piece, "row", [(0, r)])
        across = jnp.where(row_index == r, moved, across)

    part = front_cols // s.rows
    mine = lax.dynamic_slice_in_dim(across, row_index * part, part, 0)
    slot = mine
    owner = group_index // s.ratio
    for shift in range(1, s.rows):
        wanted = lax.rem(row_index + shift, s.rows)
        pairs = []
        for r in range(s.rows):
            for k in range(s.ratio):
                a, b = s.ratio * r + k, s.ratio * ((r + shift) % s.rows) + k
                index = [(g // s.cols * s.rows + r) * s.cols + g % s.cols for g in (a, b)]
                pairs.append(tuple(index))
        sent = lax.dynamic_slice_in_dim(across, wanted * part, part, 0)
        got = lax.ppermute(sent, ("front", "row", "col"), pairs)
        slot = jnp.where(owner == wanted, got, slot)
    gathered = lax.all_gather(slot, ("front", "col"))

    direct, turned = exchange(s, False, child, child_mask)
    place = jnp.stack([row_index * front_rows, group_index * front_cols]).astype(jnp.int32)
    return tuple(
        assemble_schur(
            s, slots, table, place, parent_entries, direct, turned, across, gathered
        )
    )


def solution(mesh):
    placed = (P("row", ("front", "col")), P("front", "row", "col"), P(), P("front", None, None))
    return jax.shard_map(
        functools.partial(body, mesh),
        mesh=mesh,
        in_specs=placed,
        out_specs=(P("row", ("front", "col")), P("row", None)),
        check_vma=False,
    )
```
